128 devices in a mesh: rep: 16 (over z, y_lo, core), fsdp: 8 (over y_hi, x).
Axes of the slice: x: 4, y: 4 (y_hi: 2, y_lo: 2; y = y_hi * 2 + y_lo), z: 4, core: 2. Of those that a mesh axis runs over, the one named last changes fastest.
Arguments:
- inputs: bfloat16 [16, 6144, 8192], P('rep', 'fsdp'), may hold values from -6 to 6
- targets: bfloat16 [16, 6144, 512], P('rep', 'fsdp'), may hold values from -6 to 6
- norm_gain: float32 [8192], replicated, may hold values from 0.1 to 1.9
- weights: float32 [16, 8192, 512], P('rep', 'fsdp'), may hold values from -6 to 6
- step_index: int32 [1], replicated, may hold values from 0 to 999
Outputs:
- new_weights: float32 [16, 8192, 512], P('rep', 'fsdp')
The draws below stay inside these ranges and needn't reach their ends.
All inputs are finite; a program needn't handle non-finite values.
Results may differ from the reference program's by a relative error of at most 0.015.
Values may be sent and summed in bfloat16 or wider, within the bound.
No kernel may reach another device: no remote copies, remote signals or barrier semaphores. Data moves between devices by JAX's collectives and lax.ppermute only.
A program may use at most 128 MiB of HBM per device.

```python
import jax
import jax.numpy as jnp
from jax import lax

D = 8192
TOK_DEV = 768
KW = 512
TOKENS = 6144
REPLICAS = 16
N_FSDP = 8


def shard_levels(key, dims, cuts, smallest, high):
    gain = 1.0
    for axis_at, shards_of in cuts:
        steps = jax.random.uniform(jax.random.fold_in(jax.random.fold_in(key, 6), axis_at), (shards_of,), jnp.float32, smallest / len(cuts), high / len(cuts))
        gain = gain * jnp.repeat(jnp.exp(steps), dims[axis_at] // shards_of).reshape((-1,) + (1,) * (len(dims) - 1 - axis_at))
    return gain


def gaussian(key, dims, deviation, bound, pieces=(), kind=jnp.bfloat16):
    drawn = jax.random.normal(key, dims, jnp.float32) * deviation
    if len(pieces) > 0:
        drawn = shard_levels(key, dims, pieces, -0.22, 0.18) * drawn
    return jnp.clip(drawn, min=-bound, max=bound).astype(kind)


def setup_inputs(seed: int = 0) -> dict:
    key_list = jax.random.split(jax.random.key(seed), 6)
    inputs = gaussian(key_list[0], (REPLICAS, TOKENS, D), 1.0, 6.0, ((0, 16), (1, 8)))
    targets = gaussian(key_list[1], (REPLICAS, TOKENS, KW), 1.0, 6.0, ((0, 16), (1, 8)))
    norm_gain = jnp.clip(1.0 + 0.18 * jax.random.normal(key_list[2], (D,), jnp.float32), 0.1, 1.9)
    weights = gaussian(key_list[3], (REPLICAS, D, KW), 1.0, 6.0, ((0, 16), (1, 8)), jnp.float32)
    step_index = jax.random.randint(key_list[4], (1,), 0, 1000).astype(jnp.int32)
    return {"inputs": inputs, "targets": targets, "norm_gain": norm_gain, "weights": weights, "step_index": step_index}


def replica_grad(packed):
    normed, target, master = packed
    copy = master.astype(jnp.bfloat16)
    keys = jnp.dot(normed, copy, preferred_element_type=jnp.float32) * D ** (-0.5)
    resid = (keys - target.astype(jnp.float32)).astype(jnp.bfloat16)
    blocks_h = normed.reshape(N_FSDP, TOK_DEV, D).astype(jnp.float32)
    blocks_r = resid.reshape(N_FSDP, TOK_DEV, KW).astype(jnp.float32)
    parts = jnp.einsum('btd,btk->bdk', blocks_h, blocks_r)
    return lax.optimization_barrier(jnp.sum(parts.astype(jnp.bfloat16).astype(jnp.float32), axis=0))

def reference(inputs, targets, norm_gain, weights, step_index):
    values = inputs.astype(jnp.float32)
    scale = lax.rsqrt(lax.optimization_barrier(jnp.mean(values * values, axis=-1, keepdims=True)) + 1e-05)
    normed = (values * scale * norm_gain).astype(jnp.bfloat16)
    master = weights
    rows = jnp.arange(REPLICAS, dtype=jnp.int32)
    for section in range(2):
        grad = lax.map(replica_grad, (normed, targets, master))
        half = master - 0.25 * D ** 0.5 / TOKENS * grad
        level = (step_index[0] + section) % 5
        distance = jnp.left_shift(jnp.int32(1), level.astype(jnp.int32)) % REPLICAS
        source = ((rows - distance) % REPLICAS).astype(jnp.int32)
        master = (half + jnp.take(half, source, axis=0)) * 0.5
    return master
```

```python
from functools import partial

import jax
import jax.numpy as jnp
from jax import lax
from jax.sharding import PartitionSpec as P

RING = 4
PAIR = 2
LEVELS = 5


def turn(value, reverse):
    reps, devs = lax.axis_size("rep"), lax.axis_size("fsdp")
    pairs = []
    for rep in range(reps):
        step = 1 if (rep % 2 == 0) != reverse else -1
        for dev in range(devs):
            high, low = divmod(dev, RING)
            pairs.append((rep * devs + dev, rep * devs + high * RING + (low + step) % RING))
    return lax.ppermute(value, ("rep", "fsdp"), pairs)


def swap(value):
    devs = lax.axis_size("fsdp")
    return lax.ppermute(value, "fsdp", [(dev, (dev + RING) % devs) for dev in range(devs)])


def shifted(value, distance):
    count = lax.axis_size("rep")
    return lax.ppermute(value, "rep", [(r, (r + distance) % count) for r in range(count)])


def gather_swap_first(own):
    rows = [own, swap(own)]
    blocks = [[row] for row in rows]
    for _ in range(RING - 1):
        for row in blocks:
            row.append(turn(row[-1], False))
    return blocks


def gather_turn_first(own):
    row = [own]
    for _ in range(RING - 1):
        row.append(turn(row[-1], False))
    return [row, [swap(block) for block in row]]


def add(a, b):
    return a.astype(jnp.float32) + b.astype(jnp.float32)


def scatter_turn_first(parts):
    total = []
    for row in reversed(parts):
        held = row[RING - 1]
        for m in reversed(range(RING - 1)):
            held = add(row[m], turn(held.astype(jnp.bfloat16), True))
        total.append(held)
    return total[1] + swap(total[0].astype(jnp.bfloat16)).astype(jnp.float32)


def scatter_swap_first(parts):
    row = [add(parts[0][m], swap(parts[1][m])) for m in reversed(range(RING))]
    held = row[0]
    for other in row[1:]:
        held = other + turn(held.astype(jnp.bfloat16), True).astype(jnp.float32)
    return held


def run(distances, inputs, targets, norm_gain, weights):
    tok_dev, width = inputs.shape
    key_width = targets.shape[1]
    rows = weights.shape[0]
    devs = lax.axis_size("fsdp")
    coeff = 0.25 * width**0.5 / (tok_dev * devs)
    dev = lax.axis_index("fsdp")
    high, low = dev // RING, dev % RING
    sense = 1 - 2 * (lax.axis_index("rep") % 2)

    values = inputs.astype(jnp.float32)
    scale = lax.rsqrt(jnp.mean(values * values, axis=-1, keepdims=True) + 1e-05)
    normed = []
    for a in range(PAIR):
        row = []
        for m in range(RING):
            block = (high + a) % PAIR * RING + (low - sense * m) % RING
            piece = lax.dynamic_slice_in_dim(inputs, block * rows, rows, axis=1).astype(jnp.float32)
            gain = lax.dynamic_slice_in_dim(norm_gain, block * rows, rows, axis=0)
            row.append((piece * scale * gain).astype(jnp.bfloat16))
        normed.append(row)
    normed = lax.optimization_barrier(normed)

    half_width = key_width // 2
    plans = [(gather_swap_first, scatter_turn_first), (gather_turn_first, scatter_swap_first)]
    masters = [weights[:, :half_width], weights[:, half_width:]]
    wanted = [targets[:, :half_width], targets[:, half_width:]]
    for distance in distances:
        gathered = [plan[0](m.astype(jnp.bfloat16)) for plan, m in zip(plans, masters)]
        new = []
        for plan, blocks, master, target in zip(plans, gathered, masters, wanted):
            keys = 0.0
            for a in range(PAIR):
                for m in range(RING):
                    keys += jnp.dot(normed[a][m], blocks[a][m], preferred_element_type=jnp.float32)
            resid = (keys * width**-0.5 - target.astype(jnp.float32)).astype(jnp.bfloat16)
            parts = [
                [
                    lax.dot_general(
                        normed[a][m], resid, (((0,), (0,)), ((), ())), preferred_element_type=jnp.float32
                    ).astype(jnp.bfloat16)
                    for m in range(RING)
                ]
                for a in range(PAIR)
            ]
            half = master - coeff * plan[1](parts)
            if distance == 0:
                new.append((half + half) * 0.5)
            else:
                other = shifted(half.astype(jnp.bfloat16), distance).astype(jnp.float32)
                new.append((half + other) * 0.5)
        masters = new
    return jnp.concatenate(masters, axis=1)


def local(inputs, targets, norm_gain, weights, step_index):
    replicas = lax.axis_size("rep")
    branches = []
    for level in range(LEVELS):
        distances = [2 ** ((level + step) % LEVELS) % replicas for step in range(2)]
        branches.append(partial(run, distances))
    new = lax.switch(step_index[0] % LEVELS, branches, inputs[0], targets[0], norm_gain, weights[0])
    return new[None]


def solution(mesh):
    placed = (P("rep", "fsdp", None), P("rep", "fsdp", None), P(), P("rep", "fsdp", None), P())
    return jax.shard_map(
        local, mesh=mesh, in_specs=placed, out_specs=P("rep", "fsdp", None), check_vma=False
    )
```

```python
from functools import partial

import jax
import jax.numpy as jnp
from jax import lax
from jax.sharding import PartitionSpec as P

RING = 4
PAIR = 2
LEVELS = 5
STEPS = 2
CHUNKS = 2

WAYS = ('tst', 'tst')

ORDER = (
    "10g01", "10g10", "00g01", "00g10", "10g02", "00g02", "10g03", "10g12", "10g11", "00g12", "00k10",
    "00g03", "10k10", "10k03", "00k00", "10k01", "10k00", "10k11", "00k02", "10k02", "10g13", "10k12",
    "00g11", "00k03", "00k01", "10k13", "10r", "10t13", "10s13", "00k12", "10t11", "00g13", "10t03",
    "00k11", "10s11", "10t12", "10s12", "10s03", "00k13", "00r", "00t13", "00t03", "00t11", "00s13",
    "10t10", "10s10", "00s11", "10t02", "10s02", "00t12", "00s12", "00s03", "00t10", "00s10", "10t01",
    "10s01", "00t02", "00s02", "10t00", "10z", "00t01", "00s01", "11g01", "11g10", "00t00", "00z", "11k00",
    "11k01", "11g02", "01g01", "01g10", "11g03", "11g12", "11k02", "11k10", "01g02", "01k00", "01k01",
    "11g11", "11k03", "01k10", "01g11", "01g12", "01k02", "01g03", "11k11", "11g13", "11k12", "01k11",
    "01k03", "01g13", "01k12", "11k13", "11r", "11t13", "11s13", "11t11", "11t03", "11s03", "01k13", "01r",
    "01t13", "01t11", "01t03", "01s13", "11t12", "11s12", "11s11", "01s11", "01t12", "01s12", "01s03",
    "11t10", "11s10", "11t02", "11s02", "01t10", "01s10", "01t02", "01s02", "11t01", "11s01", "01t01",
    "01s01", "11t00", "11z", "01t00", "01z",
)


def turn(value, reverse=False):
    reps, devs = lax.axis_size("rep"), lax.axis_size("fsdp")
    pairs = []
    for rep in range(reps):
        step = 1 if (rep % 2 == 0) != reverse else -1
        for dev in range(devs):
            high, low = divmod(dev, RING)
            pairs.append((rep * devs + dev, rep * devs + high * RING + (low + step) % RING))
    return lax.ppermute(value, ("rep", "fsdp"), pairs)


def swap(value):
    devs = lax.axis_size("fsdp")
    return lax.ppermute(value, "fsdp", [(dev, (dev + RING) % devs) for dev in range(devs)])


def after(value, *first):
    return lax.optimization_barrier((value, *first))[0]


def rounded(value):
    return value.astype(jnp.bfloat16)


def wide(value):
    return value.astype(jnp.float32)


def total(*values):
    return sum(wide(value) for value in values)


def moved(half, distance):
    count = lax.axis_size("rep")
    return lax.ppermute(rounded(half), "rep", [(r, (r + distance) % count) for r in range(count)])


def run(distances, inputs, targets, norm_gain, weights):
    tok_dev, width = inputs.shape
    key_width = targets.shape[1]
    rows = weights.shape[0]
    devs = lax.axis_size("fsdp")
    coeff = 0.25 * width**0.5 / (tok_dev * devs)
    dev = lax.axis_index("fsdp")
    high, low = dev // RING, dev % RING
    sense = 1 - 2 * (lax.axis_index("rep") % 2)

    pieces = []
    squares = 0.0
    for a in range(PAIR):
        for m in range(RING):
            block = (high + a) % PAIR * RING + (low - sense * m) % RING
            piece = lax.dynamic_slice_in_dim(inputs, block * rows, rows, axis=1)
            gain = lax.dynamic_slice_in_dim(norm_gain, block * rows, rows, axis=0)
            squares += jnp.sum(wide(piece) * wide(piece), axis=-1, keepdims=True)
            pieces.append((piece, gain))
    scale = lax.rsqrt(squares / width + 1e-05)
    normed = [lax.optimization_barrier(rounded(wide(piece) * scale * gain)) for piece, gain in pieces]
    normed = [normed[:RING], normed[RING:]]

    chunk = key_width // CHUNKS
    masters = [weights[:, c * chunk : (c + 1) * chunk] for c in range(CHUNKS)]
    wanted = [targets[:, c * chunk : (c + 1) * chunk] for c in range(CHUNKS)]
    sent = [rounded(master) for master in masters]
    blocks, sums, come, keys, resid, halves = {}, {}, {}, {}, {}, {}
    token = ()

    def gated(value):
        return after(value, *token) if token else value

    for name in ORDER:
        c, step, kind = int(name[0]), int(name[1]), name[2]
        at = (int(name[3]), int(name[4])) if len(name) > 3 else None
        way = (None,) + tuple(WAYS[c])
        if kind == "g":
            a, m = at
            if a == 0 or (m > 0 and way[m] == "t"):
                value, move = (sent[c] if (a, m) == (0, 1) else blocks[c, a, m - 1]), turn
            else:
                value, move = (sent[c] if m == 0 else blocks[c, 0, m]), swap
            token = (gated(value),)
            blocks[c, a, m] = move(token[0])
        elif kind == "k":
            a, m = at
            block = gated(sent[c] if at == (0, 0) else blocks[c, a, m])
            blocks[c, a, m] = block
            product = jnp.dot(normed[a][m], block, preferred_element_type=jnp.float32)
            keys[c] = keys[c] + product if c in keys else product
            token = (block, keys[c])
        elif kind == "r":
            resid[c] = rounded(keys.pop(c) * width**-0.5 - wide(wanted[c]))
            token = (resid[c],)
        elif kind == "t":
            a, m = at
            arrived = come.pop((c, a, m), [])
            if arrived:
                arrived = list(lax.optimization_barrier((*arrived, *token))[: len(arrived)])
            value = lax.dot_general(
                normed[a][m], resid[c], (((0,), (0,)), ((), ())), preferred_element_type=jnp.float32
            )
            value = total(value, *arrived)
            if at == (0, 0):
                halves[c] = masters[c] - coeff * value
                sums[c, a, m] = halves[c]
            else:
                sums[c, a, m] = rounded(value)
            token = (sums[c, a, m],)
        elif kind == "s":
            a, m = at
            value = gated(sums.pop((c, a, m)))
            token = (value,)
            if a == 0 or (m > 0 and way[m] == "t"):
                come.setdefault((c, a, m - 1), []).append(turn(value, True))
            else:
                come.setdefault((c, 0, m), []).append(swap(value))
        else:
            if distances[step] == 0:
                masters[c] = halves[c]
            else:
                masters[c] = (halves[c] + wide(moved(gated(halves[c]), distances[step]))) * 0.5
            sent[c] = rounded(masters[c])
    return jnp.concatenate(masters, axis=1)


def choose(index, first, branches, operands):
    if len(branches) == 1:
        return branches[0](*operands)
    cut = len(branches) // 2
    return lax.cond(
        index < first + cut,
        lambda *given: choose(index, first, branches[:cut], given),
        lambda *given: choose(index, first + cut, branches[cut:], given),
        *operands,
    )


def local(inputs, targets, norm_gain, weights, step_index):
    replicas = lax.axis_size("rep")
    branches = []
    for level in range(LEVELS):
        distances = [2 ** ((level + step) % LEVELS) % replicas for step in range(STEPS)]
        branches.append(partial(run, distances))
    new = choose(step_index[0] % LEVELS, 0, branches, (inputs[0], targets[0], norm_gain, weights[0]))
    return new[None]


def solution(mesh):
    placed = (P("rep", "fsdp", None), P("rep", "fsdp", None), P(), P("rep", "fsdp", None), P())
    return jax.shard_map(
        local, mesh=mesh, in_specs=placed, out_specs=P("rep", "fsdp", None), check_vma=False
    )
```

```python
from functools import partial

import jax
import jax.numpy as jnp
from jax import lax
from jax.sharding import PartitionSpec as P

RING = 4
PAIR = 2
LEVELS = 5
STEPS = 2
CHUNKS = 2

WAYS = ('tst', 'tst')

ORDER = (
    "10g01", "10g10", "00g01", "00g10", "10g02", "00g02", "10g03", "10g12", "10g11", "00g12", "00k10",
    "00g03", "10k10", "10k03", "00k00", "10k01", "10k00", "10k11", "00k02", "10k02", "10g13", "10k12",
    "00g11", "00k03", "00k01", "10k13", "10r", "10t13", "10s13", "00k12", "10t11", "00g13", "10t03",
    "00k11", "10s11", "10t12", "10s12", "10s03", "00k13", "00r", "00t13", "00t03", "00t11", "00s13",
    "10t10", "10s10", "00s11", "10t02", "10s02", "00t12", "00s12", "00s03", "00t10", "00s10", "10t01",
    "10s01", "00t02", "00s02", "10t00", "10z", "00t01", "00s01", "11g01", "11g10", "00t00", "00z", "11k00",
    "11k01", "11g02", "01g01", "01g10", "11g03", "11g12", "11k02", "11k10", "01g02", "01k00", "01k01",
    "11g11", "11k03", "01k10", "01g11", "01g12", "01k02", "01g03", "11k11", "11g13", "11k12", "01k11",
    "01k03", "01g13", "01k12", "11k13", "11r", "11t13", "11s13", "11t11", "11t03", "11s03", "01k13", "01r",
    "01t13", "01t11", "01t03", "01s13", "11t12", "11s12", "11s11", "01s11", "01t12", "01s12", "01s03",
    "11t10", "11s10", "11t02", "11s02", "01t10", "01s10", "01t02", "01s02", "11t01", "11s01", "01t01",
    "01s01", "11t00", "11z", "01t00", "01z",
)


def turn(value, reverse=False):
    reps, devs = lax.axis_size("rep"), lax.axis_size("fsdp")
    pairs = []
    for rep in range(reps):
        step = 1 if (rep % 2 == 0) != reverse else -1
        for dev in range(devs):
            high, low = divmod(dev, RING)
            pairs.append((rep * devs + dev, rep * devs + high * RING + (low + step) % RING))
    return lax.ppermute(value, ("rep", "fsdp"), pairs)


def swap(value):
    devs = lax.axis_size("fsdp")
    return lax.ppermute(value, "fsdp", [(dev, (dev + RING) % devs) for dev in range(devs)])


def after(value, *first):
    return lax.optimization_barrier((value, *first))[0]


def rounded(value):
    return value.astype(jnp.bfloat16)


def wide(value):
    return value.astype(jnp.float32)


def total(*values):
    return sum(wide(value) for value in values)


def moved(half, distance):
    count = lax.axis_size("rep")
    return lax.ppermute(rounded(half), "rep", [(r, (r + distance) % count) for r in range(count)])


def run(distances, inputs, targets, norm_gain, weights):
    tok_dev, width = inputs.shape
    key_width = targets.shape[1]
    rows = weights.shape[0]
    devs = lax.axis_size("fsdp")
    coeff = 0.25 * width**0.5 / (tok_dev * devs)
    dev = lax.axis_index("fsdp")
    high, low = dev // RING, dev % RING
    sense = 1 - 2 * (lax.axis_index("rep") % 2)

    pieces = []
    squares = 0.0
    for a in range(PAIR):
        for m in range(RING):
            block = (high + a) % PAIR * RING + (low - sense * m) % RING
            piece = lax.dynamic_slice_in_dim(inputs, block * rows, rows, axis=1)
            gain = lax.dynamic_slice_in_dim(norm_gain, block * rows, rows, axis=0)
            squares += jnp.sum(wide(piece) * wide(piece), axis=-1, keepdims=True)
            pieces.append((piece, gain))
    scale = lax.rsqrt(squares / width + 1e-05)
    normed = [lax.optimization_barrier(rounded(wide(piece) * scale * gain)) for piece, gain in pieces]
    normed = [normed[:RING], normed[RING:]]

    chunk = key_width // CHUNKS
    masters = [weights[:, c * chunk : (c + 1) * chunk] for c in range(CHUNKS)]
    wanted = [targets[:, c * chunk : (c + 1) * chunk] for c in range(CHUNKS)]
    sent = [rounded(master) for master in masters]
    blocks, sums, come, keys, resid, halves = {}, {}, {}, {}, {}, {}
    token = ()

    def gated(value):
        return after(value, *token) if token else value

    for name in ORDER:
        c, step, kind = int(name[0]), int(name[1]), name[2]
        at = (int(name[3]), int(name[4])) if len(name) > 3 else None
        way = (None,) + tuple(WAYS[c])
        if kind == "g":
            a, m = at
            if a == 0 or (m > 0 and way[m] == "t"):
                value, move = (sent[c] if (a, m) == (0, 1) else blocks[c, a, m - 1]), turn
            else:
                value, move = (sent[c] if m == 0 else blocks[c, 0, m]), swap
            token = (gated(value),)
            blocks[c, a, m] = move(token[0])
        elif kind == "k":
            a, m = at
            block = gated(sent[c] if at == (0, 0) else blocks[c, a, m])
            blocks[c, a, m] = block
            product = jnp.dot(normed[a][m], block, preferred_element_type=jnp.float32)
            keys[c] = keys[c] + product if c in keys else product
            token = (block, keys[c])
        elif kind == "r":
            resid[c] = rounded(keys.pop(c) * width**-0.5 - wide(wanted[c]))
            token = (resid[c],)
        elif kind == "t":
            a, m = at
            arrived = come.pop((c, a, m), [])
            if arrived:
                arrived = list(lax.optimization_barrier((*arrived, *token))[: len(arrived)])
            value = lax.dot_general(
                normed[a][m], resid[c], (((0,), (0,)), ((), ())), preferred_element_type=jnp.float32
            )
            value = total(value, *arrived)
            if at == (0, 0):
                halves[c] = masters[c] - coeff * value
                sums[c, a, m] = halves[c]
            else:
                sums[c, a, m] = rounded(value)
            token = (sums[c, a, m],)
        elif kind == "s":
            a, m = at
            value = gated(sums.pop((c, a, m)))
            token = (value,)
            if a == 0 or (m > 0 and way[m] == "t"):
                come.setdefault((c, a, m - 1), []).append(turn(value, True))
            else:
                come.setdefault((c, 0, m), []).append(swap(value))
        else:
            if distances[step] == 0:
                masters[c] = halves[c]
            else:
                masters[c] = (halves[c] + wide(moved(gated(halves[c]), distances[step]))) * 0.5
            sent[c] = rounded(masters[c])
    return jnp.concatenate(masters, axis=1)


def local(inputs, targets, norm_gain, weights, step_index):
    replicas = lax.axis_size("rep")
    branches = []
    for level in range(LEVELS):
        distances = [2 ** ((level + step) % LEVELS) % replicas for step in range(STEPS)]
        branches.append(partial(run, distances))
    level = step_index[0] % LEVELS
    place = jnp.where(level < 3, (level + 1) % 3, 7 - level)
    row = [branches[level] for level in (2, 0, 1, 4, 3)]
    new = lax.switch(place, row, inputs[0], targets[0], norm_gain, weights[0])
    return new[None]


def solution(mesh):
    placed = (P("rep", "fsdp", None), P("rep", "fsdp", None), P(), P("rep", "fsdp", None), P())
    return jax.shard_map(
        local, mesh=mesh, in_specs=placed, out_specs=P("rep", "fsdp", None), check_vma=False
    )
```
